128 devices in a mesh: coord: 16 (over y_lo, x, core), ex: 8 (over y_hi, z).
Axes of the slice: x: 4, y: 4 (y_hi: 2, y_lo: 2; y = y_hi * 2 + y_lo), z: 4, core: 2. Of those that a mesh axis runs over, the one named last changes fastest.
Arguments:
- gradients: bfloat16 [4096, 65536], P('ex', 'coord'), may hold values from -6 to 6
- sign_flips: int32 [65536], P('coord'), may hold values from 0 to 1
- pick_offsets: int32 [4096], P('coord'), may hold values from 0 to 4095
- queries: bfloat16 [4096, 4096], P('ex', 'coord'), may hold values from -0.09375 to 0.09375
Outputs:
- scores: float32 [4096, 4096], P('ex', 'coord')
The draws below stay inside these ranges and needn't reach their ends.
All inputs are finite; a program needn't handle non-finite values.
Results may differ from the reference program's by a relative error of at most 0.0029.
Values may be sent and summed in bfloat16 or wider, within the bound.
A program may use at most 128 MiB of HBM per device.

```python
import math
import jax
import jax.numpy as jnp
from jax import lax

COORD_DEV = 4096
SEG = 256
EX_DEV = 512
PDIM = 65536
SKETCH = 4096
EXAMPLES = 4096
NQ = 4096


def with_ends(entries, stream_key, least, largest):
    longest = entries.shape.index(max(entries.shape))
    spots = []
    for shift in (0, 1):
        where = [jax.random.randint(jax.random.fold_in(stream_key, axis), (), 0, length) for axis, length in enumerate(entries.shape)]
        where[longest] = (where[longest] + shift) % entries.shape[longest]
        spots.append(tuple(where))
    return entries.at[spots[0]].set(least).at[spots[1]].set(largest)


def block_levels(key, dims, shards, smallest, largest):
    gain, own = 1.0, jax.random.fold_in(key, 6)
    for position, blocks in shards:
        draws = jnp.exp(jax.random.uniform(jax.random.fold_in(own, position), (blocks,), jnp.float32, smallest / len(shards), largest / len(shards)))
        gain = gain * jnp.repeat(draws, dims[position] // blocks).reshape([-1 if axis == position else 1 for axis in range(len(dims))])
    return gain


def bell_draw(key, shape, width, most, cuts=(), held_as=jnp.bfloat16):
    entries = jax.random.normal(key, shape, jnp.float32) * width
    if len(cuts) > 0:
        entries = block_levels(key, shape, cuts, -0.22, 0.18) * entries
    return jnp.clip(entries, min=-most, max=most).astype(held_as)


def setup_inputs(seed: int = 0) -> dict:
    key_list = jax.random.split(jax.random.key(seed), 5)
    return {
        "gradients": bell_draw(key_list[0], (EXAMPLES, PDIM), 1.0, 6.0, ((0, 8), (1, 16))),
        "sign_flips": with_ends(jax.random.randint(key_list[1], (PDIM,), 0, 2), jax.random.fold_in(key_list[1], 1), 0, 1).astype(jnp.int32),
        "pick_offsets": with_ends(jax.random.randint(key_list[2], (SKETCH,), 0, COORD_DEV), jax.random.fold_in(key_list[2], 1), 0, COORD_DEV - 1).astype(jnp.int32),
        "queries": bell_draw(key_list[3], (NQ, SKETCH), SKETCH ** -0.5, 0.09375, ((0, 8), (1, 16))),
    }


def transform_rows(row_block, sign_values, full_picks):
    values = row_block.astype(jnp.float32) * sign_values
    total_width = values.shape[1]
    stride = 1
    for level_index in range(total_width.bit_length() - 1):
        shaped = values.reshape(values.shape[0], total_width // (2 * stride), 2, stride)
        low_half = shaped[:, :, 0:1, :]
        high_half = shaped[:, :, 1:2, :]
        values = jnp.concatenate([low_half + high_half, low_half - high_half], axis=2).reshape(values.shape[0], total_width)
        stride = stride * 2
    values = values * (1.0 / math.sqrt(total_width))
    return jnp.take(values, full_picks, axis=1).astype(jnp.bfloat16)

def reference(gradients, sign_flips, pick_offsets, queries):
    sign_values = (1 - 2 * sign_flips).astype(jnp.float32)
    full_picks = (jnp.arange(SKETCH, dtype=jnp.int32) // SEG * COORD_DEV + pick_offsets).astype(jnp.int32)
    blocks = gradients.reshape(EXAMPLES // EX_DEV, EX_DEV, PDIM)
    sketch = lax.map(lambda row_block: transform_rows(row_block, sign_values, full_picks), blocks)
    sketch = sketch.reshape(EXAMPLES, SKETCH)
    return jnp.dot(sketch, queries.T, preferred_element_type=jnp.float32)
```

```python
import math

import jax
import jax.numpy as jnp
from jax import lax
from jax.sharding import PartitionSpec as P

INNER = 128


def parity_sign(left, right, bits):
    both = left & right
    parity = jnp.zeros_like(both)
    for bit in range(bits):
        parity = parity ^ (both >> bit & 1)
    return (1 - 2 * parity).astype(jnp.bfloat16)


def body(gradients, sign_flips, pick_offsets, queries):
    n_coord = lax.axis_size("coord")
    me = lax.axis_index("coord")
    rows, width = gradients.shape
    scale = 1.0 / math.sqrt(width * n_coord)
    signed = gradients * (1 - 2 * sign_flips).astype(jnp.bfloat16)
    offsets = lax.all_gather(pick_offsets, "coord", axis=0, tiled=True)
    segment = jnp.arange(offsets.shape[0], dtype=jnp.int32) // pick_offsets.shape[0]
    outer = width // INNER
    low = parity_sign(jnp.arange(INNER, dtype=jnp.int32)[:, None], (offsets % INNER)[None, :], 7)
    high = parity_sign(jnp.arange(outer, dtype=jnp.int32)[:, None], (offsets // INNER)[None, :], 5)
    far = parity_sign(segment, me, 4)
    table = (high * far[None, :])[:, None, :] * low[None, :, :]
    table = table.reshape(width, offsets.shape[0])
    partial = jnp.dot(signed, table, preferred_element_type=jnp.float32)
    picked = lax.psum_scatter(partial, "coord", scatter_dimension=1, tiled=True) * scale
    sketch = lax.all_gather(picked.astype(jnp.bfloat16), "coord", axis=1, tiled=True)
    mine = lax.all_gather(queries, "ex", axis=0, tiled=True)
    mine = lax.all_to_all(mine, "coord", split_axis=0, concat_axis=1, tiled=True)
    return jnp.dot(sketch, mine.T, preferred_element_type=jnp.float32)


def solution(mesh):
    in_specs = (P("ex", "coord"), P("coord"), P("coord"), P("ex", "coord"))
    return jax.shard_map(body, mesh=mesh, in_specs=in_specs, out_specs=P("ex", "coord"), check_vma=False)
```

```python
import functools
import math

import jax
import jax.numpy as jnp
from jax import lax
from jax.experimental import pallas as pl
from jax.experimental.pallas import tpu as pltpu
from jax.sharding import PartitionSpec as P

MESH = pl.DeviceIdType.MESH
CHUNKS = 4
ROWS = 128
SEG = 256
INNER = 128
OUTER = 32
CHIPS = 8
RING = 4
F32 = jnp.float32
BF16 = jnp.bfloat16


def kernel(
    scale,
    grad_ref, flip_ref, off_ref, query_ref, out_ref,
    own_g, sib_g, own_flip, sib_flip, off_buf, off_smem, table, signs, image,
    picks, x1_out, x1_in, x2_out, x2_in, mid, own_x, y_out, y_in, sketch, part_out, part_in, qbuf,
    gl_sem, gs_sem, gr_sem, fs_sem, fr_sem, os_sem, or_sem, om_sem,
    x1s_sem, x1r_sem, x2s_sem, x2r_sem, ys_sem, yr_sem, as_sem, ar_sem, ps_sem, pr_sem,
    qs_sem, qr_sem, zs_sem, zr_sem,
):
    c = lax.axis_index("coord")
    e = lax.axis_index("ex")
    core = lax.rem(c, 2)
    k = lax.div(c, 2)
    x = lax.rem(k, RING)
    y = lax.div(k, RING)
    z = lax.rem(e, RING)
    yh = lax.div(e, RING)

    def chip(yy, xx):
        return yy * RING + xx

    def coord(chip_index):
        return chip_index * 2 + core

    sib = c + 1 - 2 * core
    right = lax.rem(x + 1, RING)
    left = lax.rem(x + 3, RING)
    far = lax.rem(x + 2, RING)
    xr, xl = coord(chip(y, right)), coord(chip(y, left))
    yn = coord(chip(1 - y, x))
    zr = yh * RING + lax.rem(z + 1, RING)
    zl = yh * RING + lax.rem(z + 3, RING)

    def to_coord(src, dst, ssem, rsem, who):
        return pltpu.make_async_remote_copy(
            src_ref=src, dst_ref=dst, send_sem=ssem, recv_sem=rsem,
            device_id={"coord": who}, device_id_type=MESH)

    def to_dev(src, dst, ssem, rsem, who, where):
        return pltpu.make_async_remote_copy(
            src_ref=src, dst_ref=dst, send_sem=ssem, recv_sem=rsem,
            device_id={"coord": who, "ex": where}, device_id_type=MESH)

    bar = pltpu.get_barrier_semaphore()

    def greet(who, where):
        pl.semaphore_signal(bar, inc=1, device_id={"coord": who, "ex": where}, device_id_type=MESH)

    greet(sib, e)
    greet(c, zr)
    greet(c, zl)
    for d in range(1, CHIPS):
        greet(coord(lax.rem(k + d, CHIPS)), e)
    for d in range(CHIPS):
        @pl.when(jnp.logical_or(e != k, e != d))
        def _():
            greet(coord(e), d)
        @pl.when(jnp.logical_or(e != k, k != d))
        def _():
            greet(coord(d), k)
    own_copies = []
    for q in range(CHUNKS):
        own_copies.append(pltpu.make_async_copy(grad_ref.at[pl.ds(q * ROWS, ROWS)], own_g.at[q], gl_sem.at[q]))
        own_copies[q].start()
    @pl.when(e == k)
    def _():
        pl.semaphore_wait(bar, 10 + 14)
    @pl.when(e != k)
    def _():
        pl.semaphore_wait(bar, 10 + 16)

    sends = []

    def go(copy):
        copy.start()
        sends.append(copy)
        return copy

    go(to_coord(flip_ref, sib_flip, fs_sem, fr_sem, sib))
    grad_copies = []
    grad_copies.append(go(to_coord(grad_ref.at[pl.ds(0, ROWS)], sib_g.at[0], gs_sem.at[0], gr_sem.at[0], sib)))
    for d in range(1, CHIPS):
        go(to_coord(off_ref, off_buf.at[k], os_sem.at[d], or_sem.at[k], coord(lax.rem(k + d, CHIPS))))
    own_off = pltpu.make_async_copy(off_ref, off_buf.at[k], or_sem.at[k])
    own_off.start()
    for q in range(1, CHUNKS):
        grad_copies.append(go(to_coord(grad_ref.at[pl.ds(q * ROWS, ROWS)], sib_g.at[q], gs_sem.at[q], gr_sem.at[q], sib)))
    for d in range(CHIPS):
        dz, dy = d % RING, d // RING
        piece = query_ref.at[pl.ds(dz * ROWS, ROWS)]
        here = jnp.logical_and(e == k, e == d)
        @pl.when(here)
        def _():
            pltpu.make_async_copy(piece, qbuf.at[dz, k], qr_sem.at[k]).start()
        @pl.when(jnp.logical_not(here))
        def _():
            to_dev(piece, qbuf.at[dz, k], qs_sem.at[d], qr_sem.at[k], coord(e), d).start()

    row = lax.broadcasted_iota(jnp.int32, (INNER, 2 * INNER), 0)
    col = lax.rem(lax.broadcasted_iota(jnp.int32, (INNER, 2 * INNER), 1), INNER)
    both = row & col
    both = both ^ (both >> 4)
    both = both ^ (both >> 2)
    both = both ^ (both >> 1)
    table[...] = (1 - 2 * (both & 1)).astype(F32).astype(BF16)
    signs[:, 0:INNER] = ((1 - 2 * flip_ref[...]).astype(F32) * (1 - 2 * core).astype(F32)).astype(BF16)
    to_coord(flip_ref, sib_flip, fs_sem, fr_sem, sib).wait_recv()
    signs[:, INNER:] = (1 - 2 * sib_flip[...]).astype(F32).astype(BF16)

    def transform(q):
        own_copies[q].wait()
        grad_copies[q].wait_recv()
        for a in range(OUTER):
            weight = table[...] * signs[a:a + 1, :]
            data = jnp.concatenate(
                [own_g[q, :, a * INNER:(a + 1) * INNER], sib_g[q, :, a * INNER:(a + 1) * INNER]], axis=1)
            image[a * INNER:(a + 1) * INNER, :] = lax.dot_general(
                weight, data, (((1,), (1,)), ((), ())), preferred_element_type=F32)

        @pl.loop(0, INNER // 8)
        def _(t):
            base = pl.multiple_of(t * 8, 8)
            vals = [image[pl.ds(a * INNER + base, 8), :] for a in range(OUTER)]
            h = 1
            while h < OUTER:
                vals = [vals[a] + vals[a + h] if not a & h else vals[a - h] - vals[a] for a in range(OUTER)]
                h *= 2
            for a in range(OUTER):
                image[pl.ds(a * INNER + base, 8), :] = vals[a]

    def pick(yy, xx, dst):
        seg = chip(yy, xx)

        @pl.loop(0, SEG // 32)
        def _(t):
            base = pl.multiple_of(t * 32, 32)
            for u in range(32):
                dst[pl.ds(base + u, 1), :] = image[pl.ds(off_smem[seg, 0, base + u], 1), :]

    def sign_of(yy, xx):
        odd = lax.rem(xx, 2) * lax.rem(x, 2) + lax.div(xx, 2) * lax.div(x, 2) + yy * y
        return (1 - 2 * lax.rem(odd, 2)).astype(F32)

    x1 = {}
    x2 = {}
    yc = {}
    ac = {}
    pc = {}

    def first_picks(q):
        for d in range(2):
            pick(d, far, picks)
            x1_out[q, d] = (picks[...] * sign_of(d, far)).astype(BF16)
            x1[q, d] = go(to_coord(x1_out.at[q, d], x1_in.at[q, d], x1s_sem.at[q, d], x1r_sem.at[q, d], (xr, xl)[d]))

    def send2(q, d, yy):
        x2[q, d, yy] = go(to_coord(
            x2_out.at[q, d, yy], x2_in.at[q, d, yy], x2s_sem.at[q, d, yy], x2r_sem.at[q, d, yy], (xr, xl)[d]))

    def other_picks(q):
        for d in range(2):
            xx = (right, left)[d]
            pick(1 - d, xx, picks)
            x2_out[q, d, 1 - d] = (picks[...] * sign_of(1 - d, xx)).astype(BF16)
            send2(q, d, 1 - d)
        for d in range(2):
            pick(d, (right, left)[d], mid.at[q, d])
        for yy in range(2):
            pick(yy, x, own_x.at[q, yy])

    def compute(q):
        transform(q)
        if q == 0:
            own_off.wait()
            for d in range(1, CHIPS):
                s = lax.rem(k + d, CHIPS)
                to_coord(off_ref, off_buf.at[s], os_sem.at[d], or_sem.at[s], coord(s)).wait_recv()
            om = pltpu.make_async_copy(off_buf, off_smem, om_sem)
            om.start()
            om.wait()
        first_picks(q)
        other_picks(q)

    def combine_x(q):
        for d in range(2):
            x1[q, d].wait_recv()
            x2_out[q, d, d] = (mid[q, d] * sign_of(d, (right, left)[d]) + x1_in[q, d].astype(F32)).astype(BF16)
            send2(q, d, d)

    def reduce_x(q):
        for d in range(2):
            for yy in range(2):
                x2[q, d, yy].wait_recv()
        there = 1 - y
        y_out[q] = (own_x[q, there] * sign_of(there, x)
                    + (x2_in[q, 0, there].astype(F32) + x2_in[q, 1, there].astype(F32)))
        yc[q] = go(to_coord(y_out.at[q], y_in.at[q], ys_sem.at[q], yr_sem.at[q], yn))
        own_x[q, y] = (own_x[q, y] * sign_of(y, x)
                       + (x2_in[q, 0, y].astype(F32) + x2_in[q, 1, y].astype(F32)))

    def gather_send(q, slot, n, who):
        return go(to_coord(sketch.at[q, slot], sketch.at[q, slot], as_sem.at[q, n], ar_sem.at[q, slot], who))

    def gather_wait(q, slot):
        to_coord(sketch.at[q, slot], sketch.at[q, slot], as_sem.at[q, 0], ar_sem.at[q, slot], sib).wait_recv()

    def make_sketch(q):
        yc[q].wait_recv()
        total = (own_x[q, y] + y_in[q]) * scale
        sketch[q, k] = total.T.astype(BF16)
        gather_send(q, k, 0, yn)
        gather_send(q, k, 1, xr)
        gather_send(q, k, 2, xl)

    def gather_y(q):
        slot = chip(1 - y, x)
        gather_wait(q, slot)
        gather_send(q, slot, 3, xr)
        gather_send(q, slot, 4, xl)

    def gather_x(q):
        gather_wait(q, chip(0, left))
        gather_send(q, chip(0, left), 5, xr)
        gather_wait(q, chip(1, right))
        gather_send(q, chip(1, right), 6, xl)

    def score(q):
        gather_wait(q, chip(1, left))
        gather_wait(q, chip(0, right))
        gather_wait(q, chip(0, far))
        gather_wait(q, chip(1, far))

        def half(first):
            total = None
            for s in range(CHIPS):
                rhs = jnp.concatenate([qbuf[first, s], qbuf[first + 1, s]], axis=0)
                term = lax.dot_general(sketch[q, s], rhs, (((1,), (1,)), ((), ())), preferred_element_type=F32)
                total = term if total is None else total + term
            return total

        part_out[q] = half(2 - 2 * core)
        pc[q] = go(to_coord(part_out.at[q], part_in.at[q], ps_sem.at[q], pr_sem.at[q], sib))
        out_ref[q * ROWS:(q + 1) * ROWS, :] = half(2 * core)

    def finish(q):
        pc[q].wait_recv()
        out_ref[q * ROWS:(q + 1) * ROWS, :] = out_ref[q * ROWS:(q + 1) * ROWS, :] + part_in[q]

    zw = RING * 2

    def query_ring():
        for s in range(CHIPS):
            pltpu.make_async_copy(qbuf.at[z, s], qbuf.at[z, s], qr_sem.at[s]).wait()
        go(to_dev(qbuf.at[z], qbuf.at[z], zs_sem.at[0], zr_sem.at[0], c, zr))
        go(to_dev(qbuf.at[z], qbuf.at[z], zs_sem.at[1], zr_sem.at[1], c, zl))

    half_q = CHIPS // 2

    def query_forward():
        a = lax.rem(z + 3, RING)
        b = lax.rem(z + 1, RING)
        f = lax.rem(z + 2, RING)
        to_dev(qbuf.at[a], qbuf.at[a], zs_sem.at[0], zr_sem.at[0], c, zr).wait_recv()
        lo = qbuf.at[a, pl.ds(0, half_q)]
        go(to_dev(lo, lo, zs_sem.at[2], zr_sem.at[2], c, zr))
        to_dev(qbuf.at[b], qbuf.at[b], zs_sem.at[1], zr_sem.at[1], c, zl).wait_recv()
        hi = qbuf.at[b, pl.ds(half_q, half_q)]
        go(to_dev(hi, hi, zs_sem.at[3], zr_sem.at[3], c, zl))

    def query_done():
        f = lax.rem(z + 2, RING)
        lo = qbuf.at[f, pl.ds(0, half_q)]
        to_dev(lo, lo, zs_sem.at[2], zr_sem.at[2], c, zr).wait_recv()
        hi = qbuf.at[f, pl.ds(half_q, half_q)]
        to_dev(hi, hi, zs_sem.at[3], zr_sem.at[3], c, zl).wait_recv()

    compute(0)
    query_ring()
    combine_x(0)
    compute(1)
    reduce_x(0)
    combine_x(1)
    query_forward()
    make_sketch(0)
    compute(2)
    reduce_x(1)
    gather_y(0)
    combine_x(2)
    make_sketch(1)
    gather_x(0)
    compute(3)
    reduce_x(2)
    gather_y(1)
    combine_x(3)
    make_sketch(2)
    query_done()
    score(0)
    gather_x(1)
    reduce_x(3)
    gather_y(2)
    make_sketch(3)
    score(1)
    finish(0)
    gather_x(2)
    gather_y(3)
    score(2)
    finish(1)
    gather_x(3)
    score(3)
    finish(2)
    finish(3)

    for copy in sends:
        copy.wait_send()
    for d in range(CHIPS):
        dz = d % RING
        @pl.when(jnp.logical_not(jnp.logical_and(e == k, e == d)))
        def _():
            to_dev(query_ref.at[pl.ds(dz * ROWS, ROWS)], qbuf.at[dz, k], qs_sem.at[d], qr_sem.at[k], coord(e), d).wait_send()


def body(gradients, sign_flips, pick_offsets, queries):
    rows, width = gradients.shape
    scale = 1.0 / math.sqrt(width * lax.axis_size("coord"))
    dma = pltpu.SemaphoreType.DMA
    vmem = pltpu.VMEM
    block = (SEG, ROWS)
    return pl.pallas_call(
        functools.partial(kernel, scale),
        out_shape=jax.ShapeDtypeStruct((rows, queries.shape[1]), F32),
        in_specs=[
            pl.BlockSpec(memory_space=pl.ANY),
            pl.BlockSpec(memory_space=pltpu.VMEM),
            pl.BlockSpec(memory_space=pltpu.VMEM),
            pl.BlockSpec(memory_space=pltpu.VMEM),
        ],
        out_specs=pl.BlockSpec(memory_space=pltpu.VMEM),
        scratch_shapes=[
            vmem((CHUNKS, ROWS, width), BF16),
            vmem((CHUNKS, ROWS, width), BF16),
            vmem((OUTER, INNER), jnp.int32),
            vmem((OUTER, INNER), jnp.int32),
            vmem((CHIPS, 1, SEG), jnp.int32),
            pltpu.SMEM((CHIPS, 1, SEG), jnp.int32),
            vmem((INNER, 2 * INNER), BF16),
            vmem((OUTER, 2 * INNER), BF16),
            vmem((width, ROWS), F32),
            vmem(block, F32),
            vmem((CHUNKS, 2) + block, BF16),
            vmem((CHUNKS, 2) + block, BF16),
            vmem((CHUNKS, 2, 2) + block, BF16),
            vmem((CHUNKS, 2, 2) + block, BF16),
            vmem((CHUNKS, 2) + block, F32),
            vmem((CHUNKS, 2) + block, F32),
            vmem((CHUNKS,) + block, F32),
            vmem((CHUNKS,) + block, F32),
            vmem((CHUNKS, CHIPS, ROWS, SEG), BF16),
            vmem((CHUNKS, ROWS, 256), F32),
            vmem((CHUNKS, ROWS, 256), F32),
            vmem((RING, CHIPS, ROWS, SEG), BF16),
            dma((CHUNKS,)), dma((CHUNKS,)), dma((CHUNKS,)),
            dma(()), dma(()),
            dma((CHIPS,)), dma((CHIPS,)), dma(()),
            dma((CHUNKS, 2)), dma((CHUNKS, 2)),
            dma((CHUNKS, 2, 2)), dma((CHUNKS, 2, 2)),
            dma((CHUNKS,)), dma((CHUNKS,)),
            dma((CHUNKS, 7)), dma((CHUNKS, CHIPS)),
            dma((CHUNKS,)), dma((CHUNKS,)),
            dma((CHIPS,)), dma((CHIPS,)), dma((4,)), dma((4,)),
        ],
        compiler_params=pltpu.CompilerParams(
            collective_id=0, has_side_effects=True, vmem_limit_bytes=56 << 20),
    )(gradients, sign_flips.reshape(OUTER, INNER), pick_offsets.reshape(1, SEG), queries)


def solution(mesh):
    in_specs = (P("ex", "coord"), P("coord"), P("coord"), P("ex", "coord"))
    return jax.shard_map(body, mesh=mesh, in_specs=in_specs, out_specs=P("ex", "coord"), check_vma=False)
```

```python
import functools
import math

import jax
import jax.numpy as jnp
from jax import lax
from jax.experimental import pallas as pl
from jax.experimental.pallas import tpu as pltpu
from jax.sharding import PartitionSpec as P

MESH = pl.DeviceIdType.MESH
CHUNKS = 4
ROWS = 128
SEG = 256
INNER = 128
OUTER = 32
CHIPS = 8
RING = 4
F32 = jnp.float32
BF16 = jnp.bfloat16
ORDER = (
    "T0q0A0B0C0D0T1A1B1C1X0D1",
    "T2A2X1B2r0C2D2T3R0A3X2B3",
    "R1C3D3S0X3R2S1y0b0a0w0R3",
    "S2b1a1y1f0b2a2f1S3d0f2y2",
    "b3a3M0f3F0M1y3F1M2F2M3F3",
)


def kernel(
    scale,
    grad_ref, flip_ref, off_ref, query_ref, out_ref,
    own_g, sib_g, own_flip, sib_flip, off_buf, off_smem, table, signs, image,
    picks, x1_out, x1_in, x2_out, x2_in, mid, own_x, y_out, y_in, sketch, part_out, part_in, abuf, qbuf,
    gl_sem, gs_sem, gr_sem, fs_sem, fr_sem, os_sem, or_sem, om_sem,
    x1s_sem, x1r_sem, x2s_sem, x2r_sem, ys_sem, yr_sem, as_sem, ar_sem, ps_sem, pr_sem,
    qas_sem, qar_sem, qs_sem, qr_sem, zs_sem, zr_sem,
):
    c = lax.axis_index("coord")
    e = lax.axis_index("ex")
    core = lax.rem(c, 2)
    k = lax.div(c, 2)
    x = lax.rem(k, RING)
    y = lax.div(k, RING)
    z = lax.rem(e, RING)
    yh = lax.div(e, RING)

    def chip(yy, xx):
        return yy * RING + xx

    def coord(chip_index):
        return chip_index * 2 + core

    sib = c + 1 - 2 * core
    right = lax.rem(x + 1, RING)
    left = lax.rem(x + 3, RING)
    far = lax.rem(x + 2, RING)
    xr, xl = coord(chip(y, right)), coord(chip(y, left))
    ahead = lax.rem(x + 1 + 2 * y, RING)
    behind = lax.rem(x + 3 + 2 * y, RING)
    xa, xb = coord(chip(y, ahead)), coord(chip(y, behind))
    yn = coord(chip(1 - y, x))
    zr = yh * RING + lax.rem(z + 1, RING)
    zl = yh * RING + lax.rem(z + 3, RING)

    def to_coord(src, dst, ssem, rsem, who):
        return pltpu.make_async_remote_copy(
            src_ref=src, dst_ref=dst, send_sem=ssem, recv_sem=rsem,
            device_id={"coord": who}, device_id_type=MESH)

    def to_dev(src, dst, ssem, rsem, who, where):
        return pltpu.make_async_remote_copy(
            src_ref=src, dst_ref=dst, send_sem=ssem, recv_sem=rsem,
            device_id={"coord": who, "ex": where}, device_id_type=MESH)

    bar = pltpu.get_barrier_semaphore()

    def greet(who, where):
        pl.semaphore_signal(bar, inc=1, device_id={"coord": who, "ex": where}, device_id_type=MESH)

    greet(sib, e)
    for d in range(1, RING):
        greet(c, yh * RING + lax.rem(z + d, RING))
    for d in range(1, CHIPS):
        greet(coord(lax.rem(k + d, CHIPS)), e)
    for d in range(CHIPS):
        dz, dy = d % RING, d // RING
        @pl.when(jnp.logical_or(y != yh, jnp.logical_or(x != dz, dy != yh)))
        def _():
            greet(coord(chip(yh, dz)), dy * RING + z)
        @pl.when(jnp.logical_or(y != yh, k != d))
        def _():
            greet(coord(d), y * RING + z)
    own_copies = []
    for q in range(CHUNKS):
        own_copies.append(pltpu.make_async_copy(grad_ref.at[pl.ds(q * ROWS, ROWS)], own_g.at[q], gl_sem.at[q]))
        own_copies[q].start()
    row = lax.broadcasted_iota(jnp.int32, (INNER, 2 * INNER), 0)
    col = lax.rem(lax.broadcasted_iota(jnp.int32, (INNER, 2 * INNER), 1), INNER)
    both = row & col
    both = both ^ (both >> 4)
    both = both ^ (both >> 2)
    both = both ^ (both >> 1)
    table[...] = (1 - 2 * (both & 1)).astype(F32).astype(BF16)
    signs[:, 0:INNER] = ((1 - 2 * flip_ref[...]).astype(F32) * (1 - 2 * core).astype(F32)).astype(BF16)

    @pl.when(y == yh)
    def _():
        pl.semaphore_wait(bar, 11 + 14)
    @pl.when(y != yh)
    def _():
        pl.semaphore_wait(bar, 11 + 16)

    sends = []

    def go(copy):
        copy.start()
        sends.append(copy)
        return copy

    go(to_coord(flip_ref, sib_flip, fs_sem, fr_sem, sib))
    grad_copies = []
    grad_copies.append(go(to_coord(grad_ref.at[pl.ds(0, ROWS)], sib_g.at[0], gs_sem.at[0], gr_sem.at[0], sib)))
    for d in range(1, CHIPS):
        go(to_coord(off_ref, off_buf.at[k], os_sem.at[d], or_sem.at[k], coord(lax.rem(k + d, CHIPS))))
    own_off = pltpu.make_async_copy(off_ref, off_buf.at[k], or_sem.at[k])
    own_off.start()
    for q in range(1, CHUNKS):
        grad_copies.append(go(to_coord(grad_ref.at[pl.ds(q * ROWS, ROWS)], sib_g.at[q], gs_sem.at[q], gr_sem.at[q], sib)))
    pltpu.make_async_copy(query_ref.at[pl.ds(z * ROWS, ROWS)], abuf.at[z], qar_sem.at[z]).start()
    for d in (1, 3, 2):
        zt = lax.rem(z + d, RING)
        go(to_dev(query_ref.at[pl.ds(zt * ROWS, ROWS)], abuf.at[z], qas_sem.at[d], qar_sem.at[z], c, yh * RING + zt))

    to_coord(flip_ref, sib_flip, fs_sem, fr_sem, sib).wait_recv()
    signs[:, INNER:] = (1 - 2 * sib_flip[...]).astype(F32).astype(BF16)

    def transform(q):
        own_copies[q].wait()
        grad_copies[q].wait_recv()
        for a in range(OUTER):
            weight = table[...] * signs[a:a + 1, :]
            data = jnp.concatenate(
                [own_g[q, :, a * INNER:(a + 1) * INNER], sib_g[q, :, a * INNER:(a + 1) * INNER]], axis=1)
            image[a * INNER:(a + 1) * INNER, :] = lax.dot_general(
                weight, data, (((1,), (1,)), ((), ())), preferred_element_type=F32)

        @pl.loop(0, INNER // 8)
        def _(t):
            base = pl.multiple_of(t * 8, 8)
            vals = [image[pl.ds(a * INNER + base, 8), :] for a in range(OUTER)]
            h = 1
            while h < OUTER:
                vals = [vals[a] + vals[a + h] if not a & h else vals[a - h] - vals[a] for a in range(OUTER)]
                h *= 2
            for a in range(OUTER):
                image[pl.ds(a * INNER + base, 8), :] = vals[a]

    def pick(yy, xx, dst):
        seg = chip(yy, xx)

        @pl.loop(0, SEG // 32)
        def _(t):
            base = pl.multiple_of(t * 32, 32)
            for u in range(32):
                dst[pl.ds(base + u, 1), :] = image[pl.ds(off_smem[seg, 0, base + u], 1), :]

    def sign_of(yy, xx):
        odd = lax.rem(xx, 2) * lax.rem(x, 2) + lax.div(xx, 2) * lax.div(x, 2) + yy * y
        return (1 - 2 * lax.rem(odd, 2)).astype(F32)

    x1 = {}
    x2 = {}
    yc = {}
    ac = {}
    pc = {}

    def first_picks(q):
        if q == 0:
            own_off.wait()
            for d in range(1, CHIPS):
                s = lax.rem(k + d, CHIPS)
                to_coord(off_ref, off_buf.at[s], os_sem.at[d], or_sem.at[s], coord(s)).wait_recv()
            om = pltpu.make_async_copy(off_buf, off_smem, om_sem)
            om.start()
            om.wait()
        for d in range(2):
            pick(d, far, picks)
            x1_out[q, d] = (picks[...] * sign_of(d, far)).astype(BF16)
            x1[q, d] = go(to_coord(x1_out.at[q, d], x1_in.at[q, d], x1s_sem.at[q, d], x1r_sem.at[q, d], (xr, xl)[d]))

    def send2(q, d, yy):
        x2[q, d, yy] = go(to_coord(
            x2_out.at[q, d, yy], x2_in.at[q, d, yy], x2s_sem.at[q, d, yy], x2r_sem.at[q, d, yy], (xr, xl)[d]))

    def single_picks(q):
        for d in range(2):
            xx = (right, left)[d]
            pick(1 - d, xx, picks)
            x2_out[q, d, 1 - d] = (picks[...] * sign_of(1 - d, xx)).astype(BF16)
            send2(q, d, 1 - d)

    def mid_picks(q):
        for d in range(2):
            pick(d, (right, left)[d], mid.at[q, d])

    def own_picks(q):
        for yy in range(2):
            pick(yy, x, own_x.at[q, yy])

    def combine_x(q):
        for d in range(2):
            x1[q, d].wait_recv()
            x2_out[q, d, d] = (mid[q, d] * sign_of(d, (right, left)[d]) + x1_in[q, d].astype(F32)).astype(BF16)
            send2(q, d, d)

    def reduce_x(q):
        for d in range(2):
            for yy in range(2):
                x2[q, d, yy].wait_recv()
        there = 1 - y
        y_out[q] = (own_x[q, there] * sign_of(there, x)
                    + (x2_in[q, 0, there].astype(F32) + x2_in[q, 1, there].astype(F32)))
        yc[q] = go(to_coord(y_out.at[q], y_in.at[q], ys_sem.at[q], yr_sem.at[q], yn))
        own_x[q, y] = (own_x[q, y] * sign_of(y, x)
                       + (x2_in[q, 0, y].astype(F32) + x2_in[q, 1, y].astype(F32)))

    def gather_send(q, slot, n, who):
        return go(to_coord(sketch.at[q, slot], sketch.at[q, slot], as_sem.at[q, n], ar_sem.at[q, slot], who))

    def gather_wait(q, slot):
        to_coord(sketch.at[q, slot], sketch.at[q, slot], as_sem.at[q, 0], ar_sem.at[q, slot], sib).wait_recv()

    def make_sketch(q):
        yc[q].wait_recv()
        total = (own_x[q, y] + y_in[q]) * scale
        sketch[q, k] = total.T.astype(BF16)
        gather_send(q, k, 0, yn)
        gather_send(q, k, 1, xa)
        gather_send(q, k, 2, xb)

    def gather_behind(q):
        slot = chip(y, behind)
        gather_wait(q, slot)
        gather_send(q, slot, 3, xa)

    def gather_ahead(q):
        slot = chip(y, ahead)
        gather_wait(q, slot)
        gather_send(q, slot, 4, yn)

    def gather_y(q):
        slot = chip(1 - y, x)
        gather_wait(q, slot)
        gather_send(q, slot, 5, xb)

    def gather_far(q):
        slot = chip(y, far)
        gather_wait(q, slot)
        gather_send(q, slot, 6, yn)

    def score(q):
        gather_wait(q, chip(1 - y, right))
        gather_wait(q, chip(1 - y, left))
        gather_wait(q, chip(1 - y, far))

        def half(first):
            total = None
            for s in range(CHIPS):
                rhs = jnp.concatenate([qbuf[first, s], qbuf[first + 1, s]], axis=0)
                term = lax.dot_general(sketch[q, s], rhs, (((1,), (1,)), ((), ())), preferred_element_type=F32)
                total = term if total is None else total + term
            return total

        part_out[q] = half(2 - 2 * core)
        pc[q] = go(to_coord(part_out.at[q], part_in.at[q], ps_sem.at[q], pr_sem.at[q], sib))
        out_ref[q * ROWS:(q + 1) * ROWS, :] = half(2 * core)

    def finish(q):
        pc[q].wait_recv()
        out_ref[q * ROWS:(q + 1) * ROWS, :] = out_ref[q * ROWS:(q + 1) * ROWS, :] + part_in[q]

    def query_spread(_):
        for dz in range(RING):
            pltpu.make_async_copy(abuf.at[dz], abuf.at[dz], qar_sem.at[dz]).wait()
            for dy in range(2):
                d = dy * RING + dz
                here = jnp.logical_and(y == yh, jnp.logical_and(x == dz, dy == yh))
                @pl.when(here)
                def _():
                    pltpu.make_async_copy(abuf.at[dz], qbuf.at[z, k], qr_sem.at[k]).start()
                @pl.when(jnp.logical_not(here))
                def _():
                    to_dev(abuf.at[dz], qbuf.at[z, k], qs_sem.at[d], qr_sem.at[k],
                           coord(chip(yh, dz)), dy * RING + z).start()

    def query_ring(_):
        for s in range(CHIPS):
            pltpu.make_async_copy(qbuf.at[z, s], qbuf.at[z, s], qr_sem.at[s]).wait()
        go(to_dev(qbuf.at[z], qbuf.at[z], zs_sem.at[0], zr_sem.at[0], c, zr))
        go(to_dev(qbuf.at[z], qbuf.at[z], zs_sem.at[1], zr_sem.at[1], c, zl))

    half_q = CHIPS // 2

    def query_forward(_):
        a = lax.rem(z + 3, RING)
        b = lax.rem(z + 1, RING)
        f = lax.rem(z + 2, RING)
        to_dev(qbuf.at[a], qbuf.at[a], zs_sem.at[0], zr_sem.at[0], c, zr).wait_recv()
        lo = qbuf.at[a, pl.ds(0, half_q)]
        go(to_dev(lo, lo, zs_sem.at[2], zr_sem.at[2], c, zr))
        to_dev(qbuf.at[b], qbuf.at[b], zs_sem.at[1], zr_sem.at[1], c, zl).wait_recv()
        hi = qbuf.at[b, pl.ds(half_q, half_q)]
        go(to_dev(hi, hi, zs_sem.at[3], zr_sem.at[3], c, zl))

    def query_done(_):
        f = lax.rem(z + 2, RING)
        lo = qbuf.at[f, pl.ds(0, half_q)]
        to_dev(lo, lo, zs_sem.at[2], zr_sem.at[2], c, zr).wait_recv()
        hi = qbuf.at[f, pl.ds(half_q, half_q)]
        to_dev(hi, hi, zs_sem.at[3], zr_sem.at[3], c, zl).wait_recv()

    ops = {
        "T": transform, "A": first_picks, "B": single_picks, "C": mid_picks, "D": own_picks,
        "X": combine_x, "R": reduce_x, "S": make_sketch,
        "b": gather_behind, "a": gather_ahead, "y": gather_y, "f": gather_far,
        "M": score, "F": finish, "q": query_spread, "r": query_ring, "w": query_forward, "d": query_done,
    }
    steps = "".join(ORDER)
    for i in range(0, len(steps), 2):
        ops[steps[i]](int(steps[i + 1]))

    for copy in sends:
        copy.wait_send()
    for d in range(CHIPS):
        dz, dy = d % RING, d // RING
        @pl.when(jnp.logical_or(y != yh, jnp.logical_or(x != dz, dy != yh)))
        def _():
            to_dev(abuf.at[dz], qbuf.at[z, k], qs_sem.at[d], qr_sem.at[k],
                   coord(chip(yh, dz)), dy * RING + z).wait_send()


def body(gradients, sign_flips, pick_offsets, queries):
    rows, width = gradients.shape
    scale = 1.0 / math.sqrt(width * lax.axis_size("coord"))
    dma = pltpu.SemaphoreType.DMA
    vmem = pltpu.VMEM
    block = (SEG, ROWS)
    return pl.pallas_call(
        functools.partial(kernel, scale),
        out_shape=jax.ShapeDtypeStruct((rows, queries.shape[1]), F32),
        in_specs=[
            pl.BlockSpec(memory_space=pl.ANY),
            pl.BlockSpec(memory_space=pltpu.VMEM),
            pl.BlockSpec(memory_space=pltpu.VMEM),
            pl.BlockSpec(memory_space=pl.ANY),
        ],
        out_specs=pl.BlockSpec(memory_space=pltpu.VMEM),
        scratch_shapes=[
            vmem((CHUNKS, ROWS, width), BF16),
            vmem((CHUNKS, ROWS, width), BF16),
            vmem((OUTER, INNER), jnp.int32),
            vmem((OUTER, INNER), jnp.int32),
            vmem((CHIPS, 1, SEG), jnp.int32),
            pltpu.SMEM((CHIPS, 1, SEG), jnp.int32),
            vmem((INNER, 2 * INNER), BF16),
            vmem((OUTER, 2 * INNER), BF16),
            vmem((width, ROWS), F32),
            vmem(block, F32),
            vmem((CHUNKS, 2) + block, BF16),
            vmem((CHUNKS, 2) + block, BF16),
            vmem((CHUNKS, 2, 2) + block, BF16),
            vmem((CHUNKS, 2, 2) + block, BF16),
            vmem((CHUNKS, 2) + block, F32),
            vmem((CHUNKS, 2) + block, F32),
            vmem((CHUNKS,) + block, F32),
            vmem((CHUNKS,) + block, F32),
            vmem((CHUNKS, CHIPS, ROWS, SEG), BF16),
            vmem((CHUNKS, ROWS, 256), F32),
            vmem((CHUNKS, ROWS, 256), F32),
            vmem((RING, ROWS, SEG), BF16),
            vmem((RING, CHIPS, ROWS, SEG), BF16),
            dma((CHUNKS,)), dma((CHUNKS,)), dma((CHUNKS,)),
            dma(()), dma(()),
            dma((CHIPS,)), dma((CHIPS,)), dma(()),
            dma((CHUNKS, 2)), dma((CHUNKS, 2)),
            dma((CHUNKS, 2, 2)), dma((CHUNKS, 2, 2)),
            dma((CHUNKS,)), dma((CHUNKS,)),
            dma((CHUNKS, 7)), dma((CHUNKS, CHIPS)),
            dma((CHUNKS,)), dma((CHUNKS,)),
            dma((RING,)), dma((RING,)), dma((CHIPS,)), dma((CHIPS,)), dma((4,)), dma((4,)),
        ],
        compiler_params=pltpu.CompilerParams(
            collective_id=0, has_side_effects=True, vmem_limit_bytes=56 << 20),
    )(gradients, sign_flips.reshape(OUTER, INNER), pick_offsets.reshape(1, SEG), queries)


def solution(mesh):
    in_specs = (P("ex", "coord"), P("coord"), P("coord"), P("ex", "coord"))
    return jax.shard_map(body, mesh=mesh, in_specs=in_specs, out_specs=P("ex", "coord"), check_vma=False)
```

```python
import functools
import math

import jax
import jax.numpy as jnp
from jax import lax
from jax.experimental import pallas as pl
from jax.experimental.pallas import tpu as pltpu
from jax.sharding import PartitionSpec as P

MESH = pl.DeviceIdType.MESH
CHUNKS = 4
ROWS = 128
SEG = 256
INNER = 128
OUTER = 32
CHIPS = 8
RING = 4
F32 = jnp.float32
BF16 = jnp.bfloat16
ORDER = (
    "T0A0q0B0C0D0T1A1B1C1X0D1",
    "T2A2X1B2r0C2D2T3R0A3X2B3",
    "R1C3D3S0X3R2S1y0b0a0w0R3",
    "S2b1a1y1f0b2a2f1S3d0f2y2",
    "b3a3M0f3F0M1y3F1M2F2M3F3",
)


def kernel(
    scale,
    grad_ref, flip_ref, off_ref, query_ref, out_ref,
    own_g, sib_g, own_flip, sib_flip, off_buf, off_smem, table, signs, image,
    picks, x1_out, x1_in, x2_out, x2_in, mid, own_x, y_out, y_in, sketch, part_out, part_in, abuf, qbuf,
    gl_sem, gs_sem, gr_sem, fs_sem, fr_sem, os_sem, or_sem, om_sem,
    x1s_sem, x1r_sem, x2s_sem, x2r_sem, ys_sem, yr_sem, as_sem, ar_sem, ps_sem, pr_sem,
    qas_sem, qar_sem, qs_sem, qr_sem, zs_sem, zr_sem,
):
    c = lax.axis_index("coord")
    e = lax.axis_index("ex")
    core = lax.rem(c, 2)
    k = lax.div(c, 2)
    x = lax.rem(k, RING)
    y = lax.div(k, RING)
    z = lax.rem(e, RING)
    yh = lax.div(e, RING)

    def chip(yy, xx):
        return yy * RING + xx

    def coord(chip_index):
        return chip_index * 2 + core

    sib = c + 1 - 2 * core
    right = lax.rem(x + 1, RING)
    left = lax.rem(x + 3, RING)
    far = lax.rem(x + 2, RING)
    xr, xl = coord(chip(y, right)), coord(chip(y, left))
    ahead = lax.rem(x + 1 + 2 * y, RING)
    behind = lax.rem(x + 3 + 2 * y, RING)
    xa, xb = coord(chip(y, ahead)), coord(chip(y, behind))
    yn = coord(chip(1 - y, x))
    zr = yh * RING + lax.rem(z + 1, RING)
    zl = yh * RING + lax.rem(z + 3, RING)

    def to_coord(src, dst, ssem, rsem, who):
        return pltpu.make_async_remote_copy(
            src_ref=src, dst_ref=dst, send_sem=ssem, recv_sem=rsem,
            device_id={"coord": who}, device_id_type=MESH)

    def to_dev(src, dst, ssem, rsem, who, where):
        return pltpu.make_async_remote_copy(
            src_ref=src, dst_ref=dst, send_sem=ssem, recv_sem=rsem,
            device_id={"coord": who, "ex": where}, device_id_type=MESH)

    bar = pltpu.get_barrier_semaphore()

    def greet(who, where):
        pl.semaphore_signal(bar, inc=1, device_id={"coord": who, "ex": where}, device_id_type=MESH)

    greet(sib, e)
    for d in range(1, RING):
        greet(c, yh * RING + lax.rem(z + d, RING))
    for d in range(1, CHIPS):
        greet(coord(lax.rem(k + d, CHIPS)), e)
    for d in range(CHIPS):
        dz, dy = d % RING, d // RING
        @pl.when(jnp.logical_or(y != yh, jnp.logical_or(x != dz, dy != yh)))
        def _():
            greet(coord(chip(yh, dz)), dy * RING + z)
        @pl.when(jnp.logical_or(y != yh, k != d))
        def _():
            greet(coord(d), y * RING + z)
    own_copies = []
    for q in range(CHUNKS):
        own_copies.append(pltpu.make_async_copy(grad_ref.at[pl.ds(q * ROWS, ROWS)], own_g.at[q], gl_sem.at[q]))
        own_copies[q].start()
    row = lax.broadcasted_iota(jnp.int32, (INNER, 2 * INNER), 0)
    col = lax.rem(lax.broadcasted_iota(jnp.int32, (INNER, 2 * INNER), 1), INNER)
    both = row & col
    both = both ^ (both >> 4)
    both = both ^ (both >> 2)
    both = both ^ (both >> 1)
    table[...] = (1 - 2 * (both & 1)).astype(F32).astype(BF16)
    signs[:, 0:INNER] = ((1 - 2 * flip_ref[...]).astype(F32) * (1 - 2 * core).astype(F32)).astype(BF16)

    @pl.when(y == yh)
    def _():
        pl.semaphore_wait(bar, 11 + 14)
    @pl.when(y != yh)
    def _():
        pl.semaphore_wait(bar, 11 + 16)

    sends = []

    def go(copy):
        copy.start()
        sends.append(copy)
        return copy

    go(to_coord(flip_ref, sib_flip, fs_sem, fr_sem, sib))
    grad_copies = []
    grad_copies.append(go(to_coord(grad_ref.at[pl.ds(0, ROWS)], sib_g.at[0], gs_sem.at[0], gr_sem.at[0], sib)))
    for d in range(1, CHIPS):
        go(to_coord(off_ref, off_buf.at[k], os_sem.at[d], or_sem.at[k], coord(lax.rem(k + d, CHIPS))))
    own_off = pltpu.make_async_copy(off_ref, off_buf.at[k], or_sem.at[k])
    own_off.start()
    for q in range(1, CHUNKS):
        grad_copies.append(go(to_coord(grad_ref.at[pl.ds(q * ROWS, ROWS)], sib_g.at[q], gs_sem.at[q], gr_sem.at[q], sib)))
    pltpu.make_async_copy(query_ref.at[pl.ds(z * ROWS, ROWS)], abuf.at[z], qar_sem.at[z]).start()
    for d in (1, 3, 2):
        zt = lax.rem(z + d, RING)
        go(to_dev(query_ref.at[pl.ds(zt * ROWS, ROWS)], abuf.at[z], qas_sem.at[d], qar_sem.at[z], c, yh * RING + zt))

    to_coord(flip_ref, sib_flip, fs_sem, fr_sem, sib).wait_recv()
    signs[:, INNER:] = (1 - 2 * sib_flip[...]).astype(F32).astype(BF16)

    def transform(q):
        own_copies[q].wait()
        grad_copies[q].wait_recv()
        for a in range(OUTER):
            weight = table[...] * signs[a:a + 1, :]
            data = jnp.concatenate(
                [own_g[q, :, a * INNER:(a + 1) * INNER], sib_g[q, :, a * INNER:(a + 1) * INNER]], axis=1)
            image[a * INNER:(a + 1) * INNER, :] = lax.dot_general(
                weight, data, (((1,), (1,)), ((), ())), preferred_element_type=F32)

        @pl.loop(0, INNER // 8)
        def _(t):
            base = pl.multiple_of(t * 8, 8)
            vals = [image[pl.ds(a * INNER + base, 8), :] for a in range(OUTER)]
            h = 1
            while h < OUTER:
                vals = [vals[a] + vals[a + h] if not a & h else vals[a - h] - vals[a] for a in range(OUTER)]
                h *= 2
            for a in range(OUTER):
                image[pl.ds(a * INNER + base, 8), :] = vals[a]

    def pick(yy, xx, dst):
        seg = chip(yy, xx)

        @pl.loop(0, SEG // 64)
        def _(t):
            base = pl.multiple_of(t * 64, 64)
            for u in range(64):
                dst[pl.ds(base + u, 1), :] = image[pl.ds(off_smem[seg, 0, base + u], 1), :]

    def sign_of(yy, xx):
        odd = lax.rem(xx, 2) * lax.rem(x, 2) + lax.div(xx, 2) * lax.div(x, 2) + yy * y
        return (1 - 2 * lax.rem(odd, 2)).astype(F32)

    x1 = {}
    x2 = {}
    yc = {}
    ac = {}
    pc = {}

    def first_picks(q):
        if q == 0:
            own_off.wait()
            for d in range(1, CHIPS):
                s = lax.rem(k + d, CHIPS)
                to_coord(off_ref, off_buf.at[s], os_sem.at[d], or_sem.at[s], coord(s)).wait_recv()
            om = pltpu.make_async_copy(off_buf, off_smem, om_sem)
            om.start()
            om.wait()
        for d in range(2):
            pick(d, far, picks)
            x1_out[q, d] = (picks[...] * sign_of(d, far)).astype(BF16)
            x1[q, d] = go(to_coord(x1_out.at[q, d], x1_in.at[q, d], x1s_sem.at[q, d], x1r_sem.at[q, d], (xr, xl)[d]))

    def send2(q, d, yy):
        x2[q, d, yy] = go(to_coord(
            x2_out.at[q, d, yy], x2_in.at[q, d, yy], x2s_sem.at[q, d, yy], x2r_sem.at[q, d, yy], (xr, xl)[d]))

    def single_picks(q):
        for d in range(2):
            xx = (right, left)[d]
            pick(1 - d, xx, picks)
            x2_out[q, d, 1 - d] = (picks[...] * sign_of(1 - d, xx)).astype(BF16)
            send2(q, d, 1 - d)

    def mid_picks(q):
        for d in range(2):
            pick(d, (right, left)[d], mid.at[q, d])

    def own_picks(q):
        for yy in range(2):
            pick(yy, x, own_x.at[q, yy])

    def combine_x(q):
        for d in range(2):
            x1[q, d].wait_recv()
            x2_out[q, d, d] = (mid[q, d] * sign_of(d, (right, left)[d]) + x1_in[q, d].astype(F32)).astype(BF16)
            send2(q, d, d)

    def reduce_x(q):
        for d in range(2):
            for yy in range(2):
                x2[q, d, yy].wait_recv()
        there = 1 - y
        y_out[q] = (own_x[q, there] * sign_of(there, x)
                    + (x2_in[q, 0, there].astype(F32) + x2_in[q, 1, there].astype(F32)))
        yc[q] = go(to_coord(y_out.at[q], y_in.at[q], ys_sem.at[q], yr_sem.at[q], yn))
        own_x[q, y] = (own_x[q, y] * sign_of(y, x)
                       + (x2_in[q, 0, y].astype(F32) + x2_in[q, 1, y].astype(F32)))

    def gather_send(q, slot, n, who):
        return go(to_coord(sketch.at[q, slot], sketch.at[q, slot], as_sem.at[q, n], ar_sem.at[q, slot], who))

    def gather_wait(q, slot):
        to_coord(sketch.at[q, slot], sketch.at[q, slot], as_sem.at[q, 0], ar_sem.at[q, slot], sib).wait_recv()

    def make_sketch(q):
        yc[q].wait_recv()
        total = (own_x[q, y] + y_in[q]) * scale
        sketch[q, k] = total.T.astype(BF16)
        gather_send(q, k, 0, yn)
        gather_send(q, k, 1, xa)
        gather_send(q, k, 2, xb)

    def gather_behind(q):
        slot = chip(y, behind)
        gather_wait(q, slot)
        gather_send(q, slot, 3, xa)

    def gather_ahead(q):
        slot = chip(y, ahead)
        gather_wait(q, slot)
        gather_send(q, slot, 4, yn)

    def gather_y(q):
        slot = chip(1 - y, x)
        gather_wait(q, slot)
        gather_send(q, slot, 5, xb)

    def gather_far(q):
        slot = chip(y, far)
        gather_wait(q, slot)
        gather_send(q, slot, 6, yn)

    def score(q):
        gather_wait(q, chip(1 - y, right))
        gather_wait(q, chip(1 - y, left))
        gather_wait(q, chip(1 - y, far))

        def half(first):
            total = None
            for s in range(CHIPS):
                rhs = jnp.concatenate([qbuf[first, s], qbuf[first + 1, s]], axis=0)
                term = lax.dot_general(sketch[q, s], rhs, (((1,), (1,)), ((), ())), preferred_element_type=F32)
                total = term if total is None else total + term
            return total

        part_out[q] = half(2 - 2 * core)
        pc[q] = go(to_coord(part_out.at[q], part_in.at[q], ps_sem.at[q], pr_sem.at[q], sib))
        out_ref[q * ROWS:(q + 1) * ROWS, :] = half(2 * core)

    def finish(q):
        pc[q].wait_recv()
        out_ref[q * ROWS:(q + 1) * ROWS, :] = out_ref[q * ROWS:(q + 1) * ROWS, :] + part_in[q]

    def query_spread(_):
        for dz in range(RING):
            pltpu.make_async_copy(abuf.at[dz], abuf.at[dz], qar_sem.at[dz]).wait()
            for dy in range(2):
                d = dy * RING + dz
                here = jnp.logical_and(y == yh, jnp.logical_and(x == dz, dy == yh))
                @pl.when(here)
                def _():
                    pltpu.make_async_copy(abuf.at[dz], qbuf.at[z, k], qr_sem.at[k]).start()
                @pl.when(jnp.logical_not(here))
                def _():
                    to_dev(abuf.at[dz], qbuf.at[z, k], qs_sem.at[d], qr_sem.at[k],
                           coord(chip(yh, dz)), dy * RING + z).start()

    def query_ring(_):
        for s in range(CHIPS):
            pltpu.make_async_copy(qbuf.at[z, s], qbuf.at[z, s], qr_sem.at[s]).wait()
        go(to_dev(qbuf.at[z], qbuf.at[z], zs_sem.at[0], zr_sem.at[0], c, zr))
        go(to_dev(qbuf.at[z], qbuf.at[z], zs_sem.at[1], zr_sem.at[1], c, zl))

    half_q = CHIPS // 2

    def query_forward(_):
        a = lax.rem(z + 3, RING)
        b = lax.rem(z + 1, RING)
        f = lax.rem(z + 2, RING)
        to_dev(qbuf.at[a], qbuf.at[a], zs_sem.at[0], zr_sem.at[0], c, zr).wait_recv()
        lo = qbuf.at[a, pl.ds(0, half_q)]
        go(to_dev(lo, lo, zs_sem.at[2], zr_sem.at[2], c, zr))
        to_dev(qbuf.at[b], qbuf.at[b], zs_sem.at[1], zr_sem.at[1], c, zl).wait_recv()
        hi = qbuf.at[b, pl.ds(half_q, half_q)]
        go(to_dev(hi, hi, zs_sem.at[3], zr_sem.at[3], c, zl))

    def query_done(_):
        f = lax.rem(z + 2, RING)
        lo = qbuf.at[f, pl.ds(0, half_q)]
        to_dev(lo, lo, zs_sem.at[2], zr_sem.at[2], c, zr).wait_recv()
        hi = qbuf.at[f, pl.ds(half_q, half_q)]
        to_dev(hi, hi, zs_sem.at[3], zr_sem.at[3], c, zl).wait_recv()

    ops = {
        "T": transform, "A": first_picks, "B": single_picks, "C": mid_picks, "D": own_picks,
        "X": combine_x, "R": reduce_x, "S": make_sketch,
        "b": gather_behind, "a": gather_ahead, "y": gather_y, "f": gather_far,
        "M": score, "F": finish, "q": query_spread, "r": query_ring, "w": query_forward, "d": query_done,
    }
    steps = "".join(ORDER)
    for i in range(0, len(steps), 2):
        ops[steps[i]](int(steps[i + 1]))

    for copy in sends:
        copy.wait_send()
    for d in range(CHIPS):
        dz, dy = d % RING, d // RING
        @pl.when(jnp.logical_or(y != yh, jnp.logical_or(x != dz, dy != yh)))
        def _():
            to_dev(abuf.at[dz], qbuf.at[z, k], qs_sem.at[d], qr_sem.at[k],
                   coord(chip(yh, dz)), dy * RING + z).wait_send()


def body(gradients, sign_flips, pick_offsets, queries):
    rows, width = gradients.shape
    scale = 1.0 / math.sqrt(width * lax.axis_size("coord"))
    dma = pltpu.SemaphoreType.DMA
    vmem = pltpu.VMEM
    block = (SEG, ROWS)
    return pl.pallas_call(
        functools.partial(kernel, scale),
        out_shape=jax.ShapeDtypeStruct((rows, queries.shape[1]), F32),
        in_specs=[
            pl.BlockSpec(memory_space=pl.ANY),
            pl.BlockSpec(memory_space=pltpu.VMEM),
            pl.BlockSpec(memory_space=pltpu.VMEM),
            pl.BlockSpec(memory_space=pl.ANY),
        ],
        out_specs=pl.BlockSpec(memory_space=pltpu.VMEM),
        scratch_shapes=[
            vmem((CHUNKS, ROWS, width), BF16),
            vmem((CHUNKS, ROWS, width), BF16),
            vmem((OUTER, INNER), jnp.int32),
            vmem((OUTER, INNER), jnp.int32),
            vmem((CHIPS, 1, SEG), jnp.int32),
            pltpu.SMEM((CHIPS, 1, SEG), jnp.int32),
            vmem((INNER, 2 * INNER), BF16),
            vmem((OUTER, 2 * INNER), BF16),
            vmem((width, ROWS), F32),
            vmem(block, F32),
            vmem((CHUNKS, 2) + block, BF16),
            vmem((CHUNKS, 2) + block, BF16),
            vmem((CHUNKS, 2, 2) + block, BF16),
            vmem((CHUNKS, 2, 2) + block, BF16),
            vmem((CHUNKS, 2) + block, F32),
            vmem((CHUNKS, 2) + block, F32),
            vmem((CHUNKS,) + block, F32),
            vmem((CHUNKS,) + block, F32),
            vmem((CHUNKS, CHIPS, ROWS, SEG), BF16),
            vmem((CHUNKS, ROWS, 256), F32),
            vmem((CHUNKS, ROWS, 256), F32),
            vmem((RING, ROWS, SEG), BF16),
            vmem((RING, CHIPS, ROWS, SEG), BF16),
            dma((CHUNKS,)), dma((CHUNKS,)), dma((CHUNKS,)),
            dma(()), dma(()),
            dma((CHIPS,)), dma((CHIPS,)), dma(()),
            dma((CHUNKS, 2)), dma((CHUNKS, 2)),
            dma((CHUNKS, 2, 2)), dma((CHUNKS, 2, 2)),
            dma((CHUNKS,)), dma((CHUNKS,)),
            dma((CHUNKS, 7)), dma((CHUNKS, CHIPS)),
            dma((CHUNKS,)), dma((CHUNKS,)),
            dma((RING,)), dma((RING,)), dma((CHIPS,)), dma((CHIPS,)), dma((4,)), dma((4,)),
        ],
        compiler_params=pltpu.CompilerParams(
            collective_id=0, has_side_effects=True, vmem_limit_bytes=56 << 20),
    )(gradients, sign_flips.reshape(OUTER, INNER), pick_offsets.reshape(1, SEG), queries)


def solution(mesh):
    in_specs = (P("ex", "coord"), P("coord"), P("coord"), P("ex", "coord"))
    return jax.shard_map(body, mesh=mesh, in_specs=in_specs, out_specs=P("ex", "coord"), check_vma=False)
```

```python
import functools
import math

import jax
import jax.numpy as jnp
from jax import lax
from jax.experimental import pallas as pl
from jax.experimental.pallas import tpu as pltpu
from jax.sharding import PartitionSpec as P

MESH = pl.DeviceIdType.MESH
CHUNKS = 4
ROWS = 128
SEG = 256
INNER = 128
OUTER = 32
CHIPS = 8
RING = 4
F32 = jnp.float32
BF16 = jnp.bfloat16
ORDER = (
    "T0A0q0B0C0D0T1A1B1C1X0D1",
    "T2A2X1B2r0C2D2R0T3A3X2B3",
    "R1C3D3S0X3R2S1y0b0a0w0R3",
    "S2b1a1y1f0b2a2f1S3d0f2y2",
    "b3a3M0f3F0M1y3F1M2F2M3F3",
)


def kernel(
    scale,
    grad_ref, flip_ref, off_ref, query_ref, out_ref,
    own_g, sib_g, own_flip, sib_flip, off_buf, off_smem, table, signs, image,
    picks, x1_out, x1_in, x2_out, x2_in, mid, own_x, y_out, y_in, sketch, part_out, part_in, abuf, qbuf,
    gl_sem, gs_sem, gr_sem, fs_sem, fr_sem, os_sem, or_sem, om_sem,
    x1s_sem, x1r_sem, x2s_sem, x2r_sem, ys_sem, yr_sem, as_sem, ar_sem, ps_sem, pr_sem,
    qas_sem, qar_sem, qs_sem, qr_sem, zs_sem, zr_sem,
):
    c = lax.axis_index("coord")
    e = lax.axis_index("ex")
    core = lax.rem(c, 2)
    k = lax.div(c, 2)
    x = lax.rem(k, RING)
    y = lax.div(k, RING)
    z = lax.rem(e, RING)
    yh = lax.div(e, RING)

    def chip(yy, xx):
        return yy * RING + xx

    def coord(chip_index):
        return chip_index * 2 + core

    sib = c + 1 - 2 * core
    right = lax.rem(x + 1, RING)
    left = lax.rem(x + 3, RING)
    far = lax.rem(x + 2, RING)
    xr, xl = coord(chip(y, right)), coord(chip(y, left))
    ahead = lax.rem(x + 1 + 2 * y, RING)
    behind = lax.rem(x + 3 + 2 * y, RING)
    xa, xb = coord(chip(y, ahead)), coord(chip(y, behind))
    yn = coord(chip(1 - y, x))
    zr = yh * RING + lax.rem(z + 1, RING)
    zl = yh * RING + lax.rem(z + 3, RING)

    def to_coord(src, dst, ssem, rsem, who):
        return pltpu.make_async_remote_copy(
            src_ref=src, dst_ref=dst, send_sem=ssem, recv_sem=rsem,
            device_id={"coord": who}, device_id_type=MESH)

    def to_dev(src, dst, ssem, rsem, who, where):
        return pltpu.make_async_remote_copy(
            src_ref=src, dst_ref=dst, send_sem=ssem, recv_sem=rsem,
            device_id={"coord": who, "ex": where}, device_id_type=MESH)

    bar = pltpu.get_barrier_semaphore()

    def greet(who, where):
        pl.semaphore_signal(bar, inc=1, device_id={"coord": who, "ex": where}, device_id_type=MESH)

    greet(sib, e)
    for d in range(1, RING):
        greet(c, yh * RING + lax.rem(z + d, RING))
    for d in range(1, CHIPS):
        greet(coord(lax.rem(k + d, CHIPS)), e)
    for d in range(CHIPS):
        dz, dy = d % RING, d // RING
        @pl.when(jnp.logical_or(y != yh, jnp.logical_or(x != dz, dy != yh)))
        def _():
            greet(coord(chip(yh, dz)), dy * RING + z)
        @pl.when(jnp.logical_or(y != yh, k != d))
        def _():
            greet(coord(d), y * RING + z)
    own_copies = []
    for q in range(CHUNKS):
        own_copies.append(pltpu.make_async_copy(grad_ref.at[pl.ds(q * ROWS, ROWS)], own_g.at[q], gl_sem.at[q]))
        own_copies[q].start()
    row = lax.broadcasted_iota(jnp.int32, (INNER, 2 * INNER), 0)
    col = lax.rem(lax.broadcasted_iota(jnp.int32, (INNER, 2 * INNER), 1), INNER)
    both = row & col
    both = both ^ (both >> 4)
    both = both ^ (both >> 2)
    both = both ^ (both >> 1)
    table[...] = (1 - 2 * (both & 1)).astype(F32).astype(BF16)
    signs[:, 0:INNER] = ((1 - 2 * flip_ref[...]).astype(F32) * (1 - 2 * core).astype(F32)).astype(BF16)

    @pl.when(y == yh)
    def _():
        pl.semaphore_wait(bar, 11 + 14)
    @pl.when(y != yh)
    def _():
        pl.semaphore_wait(bar, 11 + 16)

    sends = []

    def go(copy):
        copy.start()
        sends.append(copy)
        return copy

    go(to_coord(flip_ref, sib_flip, fs_sem, fr_sem, sib))
    grad_copies = []
    grad_copies.append(go(to_coord(grad_ref.at[pl.ds(0, ROWS)], sib_g.at[0], gs_sem.at[0], gr_sem.at[0], sib)))
    for d in range(1, CHIPS):
        go(to_coord(off_ref, off_buf.at[k], os_sem.at[d], or_sem.at[k], coord(lax.rem(k + d, CHIPS))))
    own_off = pltpu.make_async_copy(off_ref, off_buf.at[k], or_sem.at[k])
    own_off.start()
    for q in range(1, CHUNKS):
        grad_copies.append(go(to_coord(grad_ref.at[pl.ds(q * ROWS, ROWS)], sib_g.at[q], gs_sem.at[q], gr_sem.at[q], sib)))
    pltpu.make_async_copy(query_ref.at[pl.ds(z * ROWS, ROWS)], abuf.at[z], qar_sem.at[z]).start()
    for d in (1, 3, 2):
        zt = lax.rem(z + d, RING)
        go(to_dev(query_ref.at[pl.ds(zt * ROWS, ROWS)], abuf.at[z], qas_sem.at[d], qar_sem.at[z], c, yh * RING + zt))

    to_coord(flip_ref, sib_flip, fs_sem, fr_sem, sib).wait_recv()
    signs[:, INNER:] = (1 - 2 * sib_flip[...]).astype(F32).astype(BF16)

    def transform(q):
        own_copies[q].wait()
        grad_copies[q].wait_recv()
        for a in range(OUTER):
            weight = table[...] * signs[a:a + 1, :]
            data = jnp.concatenate(
                [own_g[q, :, a * INNER:(a + 1) * INNER], sib_g[q, :, a * INNER:(a + 1) * INNER]], axis=1)
            image[a * INNER:(a + 1) * INNER, :] = lax.dot_general(
                weight, data, (((1,), (1,)), ((), ())), preferred_element_type=F32)

        @pl.loop(0, INNER // 8)
        def _(t):
            base = pl.multiple_of(t * 8, 8)
            vals = [image[pl.ds(a * INNER + base, 8), :] for a in range(OUTER)]
            h = 1
            while h < OUTER:
                vals = [vals[a] + vals[a + h] if not a & h else vals[a - h] - vals[a] for a in range(OUTER)]
                h *= 2
            for a in range(OUTER):
                image[pl.ds(a * INNER + base, 8), :] = vals[a]

    def pick(yy, xx, dst):
        seg = chip(yy, xx)

        @pl.loop(0, SEG // 64)
        def _(t):
            base = pl.multiple_of(t * 64, 64)
            for u in range(64):
                dst[pl.ds(base + u, 1), :] = image[pl.ds(off_smem[seg, 0, base + u], 1), :]

    def sign_of(yy, xx):
        odd = lax.rem(xx, 2) * lax.rem(x, 2) + lax.div(xx, 2) * lax.div(x, 2) + yy * y
        return (1 - 2 * lax.rem(odd, 2)).astype(F32)

    x1 = {}
    x2 = {}
    yc = {}
    ac = {}
    pc = {}

    def first_picks(q):
        if q == 0:
            own_off.wait()
            for d in range(1, CHIPS):
                s = lax.rem(k + d, CHIPS)
                to_coord(off_ref, off_buf.at[s], os_sem.at[d], or_sem.at[s], coord(s)).wait_recv()
            om = pltpu.make_async_copy(off_buf, off_smem, om_sem)
            om.start()
            om.wait()
        for d in range(2):
            pick(d, far, picks)
            x1_out[q, d] = (picks[...] * sign_of(d, far)).astype(BF16)
            x1[q, d] = go(to_coord(x1_out.at[q, d], x1_in.at[q, d], x1s_sem.at[q, d], x1r_sem.at[q, d], (xr, xl)[d]))

    def send2(q, d, yy):
        x2[q, d, yy] = go(to_coord(
            x2_out.at[q, d, yy], x2_in.at[q, d, yy], x2s_sem.at[q, d, yy], x2r_sem.at[q, d, yy], (xr, xl)[d]))

    def single_picks(q):
        for d in range(2):
            xx = (right, left)[d]
            pick(1 - d, xx, picks)
            x2_out[q, d, 1 - d] = (picks[...] * sign_of(1 - d, xx)).astype(BF16)
            send2(q, d, 1 - d)

    def mid_picks(q):
        for d in range(2):
            pick(d, (right, left)[d], mid.at[q, d])

    def own_picks(q):
        for yy in range(2):
            pick(yy, x, own_x.at[q, yy])

    def combine_x(q):
        for d in range(2):
            x1[q, d].wait_recv()
            x2_out[q, d, d] = (mid[q, d] * sign_of(d, (right, left)[d]) + x1_in[q, d].astype(F32)).astype(BF16)
            send2(q, d, d)

    def reduce_x(q):
        for d in range(2):
            for yy in range(2):
                x2[q, d, yy].wait_recv()
        there = 1 - y
        y_out[q] = (own_x[q, there] * sign_of(there, x)
                    + (x2_in[q, 0, there].astype(F32) + x2_in[q, 1, there].astype(F32)))
        yc[q] = go(to_coord(y_out.at[q], y_in.at[q], ys_sem.at[q], yr_sem.at[q], yn))
        own_x[q, y] = (own_x[q, y] * sign_of(y, x)
                       + (x2_in[q, 0, y].astype(F32) + x2_in[q, 1, y].astype(F32)))

    def gather_send(q, slot, n, who):
        return go(to_coord(sketch.at[q, slot], sketch.at[q, slot], as_sem.at[q, n], ar_sem.at[q, slot], who))

    def gather_wait(q, slot):
        to_coord(sketch.at[q, slot], sketch.at[q, slot], as_sem.at[q, 0], ar_sem.at[q, slot], sib).wait_recv()

    def make_sketch(q):
        yc[q].wait_recv()
        total = (own_x[q, y] + y_in[q]) * scale
        sketch[q, k] = total.T.astype(BF16)
        gather_send(q, k, 0, yn)
        gather_send(q, k, 1, xa)
        gather_send(q, k, 2, xb)

    def gather_behind(q):
        slot = chip(y, behind)
        gather_wait(q, slot)
        gather_send(q, slot, 3, xa)

    def gather_ahead(q):
        slot = chip(y, ahead)
        gather_wait(q, slot)
        gather_send(q, slot, 4, yn)

    def gather_y(q):
        slot = chip(1 - y, x)
        gather_wait(q, slot)
        gather_send(q, slot, 5, xb)

    def gather_far(q):
        slot = chip(y, far)
        gather_wait(q, slot)
        gather_send(q, slot, 6, yn)

    def score(q):
        gather_wait(q, chip(1 - y, right))
        gather_wait(q, chip(1 - y, left))
        gather_wait(q, chip(1 - y, far))

        def half(first):
            total = None
            for s in range(CHIPS):
                rhs = jnp.concatenate([qbuf[first, s], qbuf[first + 1, s]], axis=0)
                term = lax.dot_general(sketch[q, s], rhs, (((1,), (1,)), ((), ())), preferred_element_type=F32)
                total = term if total is None else total + term
            return total

        part_out[q] = half(2 - 2 * core)
        pc[q] = go(to_coord(part_out.at[q], part_in.at[q], ps_sem.at[q], pr_sem.at[q], sib))
        out_ref[q * ROWS:(q + 1) * ROWS, :] = half(2 * core)

    def finish(q):
        pc[q].wait_recv()
        out_ref[q * ROWS:(q + 1) * ROWS, :] = out_ref[q * ROWS:(q + 1) * ROWS, :] + part_in[q]

    def query_spread(_):
        for dz in range(RING):
            pltpu.make_async_copy(abuf.at[dz], abuf.at[dz], qar_sem.at[dz]).wait()
            for dy in range(2):
                d = dy * RING + dz
                here = jnp.logical_and(y == yh, jnp.logical_and(x == dz, dy == yh))
                @pl.when(here)
                def _():
                    pltpu.make_async_copy(abuf.at[dz], qbuf.at[z, k], qr_sem.at[k]).start()
                @pl.when(jnp.logical_not(here))
                def _():
                    to_dev(abuf.at[dz], qbuf.at[z, k], qs_sem.at[d], qr_sem.at[k],
                           coord(chip(yh, dz)), dy * RING + z).start()

    def query_ring(_):
        for s in range(CHIPS):
            pltpu.make_async_copy(qbuf.at[z, s], qbuf.at[z, s], qr_sem.at[s]).wait()
        go(to_dev(qbuf.at[z], qbuf.at[z], zs_sem.at[0], zr_sem.at[0], c, zr))
        go(to_dev(qbuf.at[z], qbuf.at[z], zs_sem.at[1], zr_sem.at[1], c, zl))

    half_q = CHIPS // 2

    def query_forward(_):
        a = lax.rem(z + 3, RING)
        b = lax.rem(z + 1, RING)
        f = lax.rem(z + 2, RING)
        to_dev(qbuf.at[a], qbuf.at[a], zs_sem.at[0], zr_sem.at[0], c, zr).wait_recv()
        lo = qbuf.at[a, pl.ds(0, half_q)]
        go(to_dev(lo, lo, zs_sem.at[2], zr_sem.at[2], c, zr))
        to_dev(qbuf.at[b], qbuf.at[b], zs_sem.at[1], zr_sem.at[1], c, zl).wait_recv()
        hi = qbuf.at[b, pl.ds(half_q, half_q)]
        go(to_dev(hi, hi, zs_sem.at[3], zr_sem.at[3], c, zl))

    def query_done(_):
        f = lax.rem(z + 2, RING)
        lo = qbuf.at[f, pl.ds(0, half_q)]
        to_dev(lo, lo, zs_sem.at[2], zr_sem.at[2], c, zr).wait_recv()
        hi = qbuf.at[f, pl.ds(half_q, half_q)]
        to_dev(hi, hi, zs_sem.at[3], zr_sem.at[3], c, zl).wait_recv()

    ops = {
        "T": transform, "A": first_picks, "B": single_picks, "C": mid_picks, "D": own_picks,
        "X": combine_x, "R": reduce_x, "S": make_sketch,
        "b": gather_behind, "a": gather_ahead, "y": gather_y, "f": gather_far,
        "M": score, "F": finish, "q": query_spread, "r": query_ring, "w": query_forward, "d": query_done,
    }
    steps = "".join(ORDER)
    for i in range(0, len(steps), 2):
        ops[steps[i]](int(steps[i + 1]))

    for copy in sends:
        copy.wait_send()
    for d in range(CHIPS):
        dz, dy = d % RING, d // RING
        @pl.when(jnp.logical_or(y != yh, jnp.logical_or(x != dz, dy != yh)))
        def _():
            to_dev(abuf.at[dz], qbuf.at[z, k], qs_sem.at[d], qr_sem.at[k],
                   coord(chip(yh, dz)), dy * RING + z).wait_send()


def body(gradients, sign_flips, pick_offsets, queries):
    rows, width = gradients.shape
    scale = 1.0 / math.sqrt(width * lax.axis_size("coord"))
    dma = pltpu.SemaphoreType.DMA
    vmem = pltpu.VMEM
    block = (SEG, ROWS)
    return pl.pallas_call(
        functools.partial(kernel, scale),
        out_shape=jax.ShapeDtypeStruct((rows, queries.shape[1]), F32),
        in_specs=[
            pl.BlockSpec(memory_space=pl.ANY),
            pl.BlockSpec(memory_space=pltpu.VMEM),
            pl.BlockSpec(memory_space=pltpu.VMEM),
            pl.BlockSpec(memory_space=pl.ANY),
        ],
        out_specs=pl.BlockSpec(memory_space=pltpu.VMEM),
        scratch_shapes=[
            vmem((CHUNKS, ROWS, width), BF16),
            vmem((CHUNKS, ROWS, width), BF16),
            vmem((OUTER, INNER), jnp.int32),
            vmem((OUTER, INNER), jnp.int32),
            vmem((CHIPS, 1, SEG), jnp.int32),
            pltpu.SMEM((CHIPS, 1, SEG), jnp.int32),
            vmem((INNER, 2 * INNER), BF16),
            vmem((OUTER, 2 * INNER), BF16),
            vmem((width, ROWS), F32),
            vmem(block, F32),
            vmem((CHUNKS, 2) + block, BF16),
            vmem((CHUNKS, 2) + block, BF16),
            vmem((CHUNKS, 2, 2) + block, BF16),
            vmem((CHUNKS, 2, 2) + block, BF16),
            vmem((CHUNKS, 2) + block, F32),
            vmem((CHUNKS, 2) + block, F32),
            vmem((CHUNKS,) + block, F32),
            vmem((CHUNKS,) + block, F32),
            vmem((CHUNKS, CHIPS, ROWS, SEG), BF16),
            vmem((CHUNKS, ROWS, 256), F32),
            vmem((CHUNKS, ROWS, 256), F32),
            vmem((RING, ROWS, SEG), BF16),
            vmem((RING, CHIPS, ROWS, SEG), BF16),
            dma((CHUNKS,)), dma((CHUNKS,)), dma((CHUNKS,)),
            dma(()), dma(()),
            dma((CHIPS,)), dma((CHIPS,)), dma(()),
            dma((CHUNKS, 2)), dma((CHUNKS, 2)),
            dma((CHUNKS, 2, 2)), dma((CHUNKS, 2, 2)),
            dma((CHUNKS,)), dma((CHUNKS,)),
            dma((CHUNKS, 7)), dma((CHUNKS, CHIPS)),
            dma((CHUNKS,)), dma((CHUNKS,)),
            dma((RING,)), dma((RING,)), dma((CHIPS,)), dma((CHIPS,)), dma((4,)), dma((4,)),
        ],
        compiler_params=pltpu.CompilerParams(
            collective_id=0, has_side_effects=True, vmem_limit_bytes=56 << 20),
    )(gradients, sign_flips.reshape(OUTER, INNER), pick_offsets.reshape(1, SEG), queries)


def solution(mesh):
    in_specs = (P("ex", "coord"), P("coord"), P("coord"), P("ex", "coord"))
    return jax.shard_map(body, mesh=mesh, in_specs=in_specs, out_specs=P("ex", "coord"), check_vma=False)
```
